32 devices in a mesh: seq: 8 (over z, x), fsdp: 4 (over y, core).
Axes of the slice: x: 2, y: 2, z: 4, core: 2. Of those that a mesh axis runs over, the one named last changes fastest.
Arguments:
- inputs: bfloat16 [4, 2048, 1536], P(None, ('seq', 'fsdp')), may hold values from -6 to 6
- cotangent: bfloat16 [4, 2048, 1536], P(None, ('seq', 'fsdp')), may hold values from -6 to 6
- dilated_kernel_weight: bfloat16 [1536, 3, 768], P('seq', None, 'fsdp'), may hold values from -0.09375 to 0.09375
- point_weight: bfloat16 [1536, 768], P('seq', 'fsdp'), may hold values from -0.21875 to 0.21875
Outputs:
- outputs: bfloat16 [4, 2048, 1536], P(None, ('seq', 'fsdp'))
- grad_inputs: bfloat16 [4, 2048, 1536], P(None, ('seq', 'fsdp'))
- grad_conv: float32 [1536, 3, 768], P('seq', None, 'fsdp')
- grad_point: float32 [1536, 768], P('seq', 'fsdp')
The draws below stay inside these ranges and needn't reach their ends.
All inputs are finite; a program needn't handle non-finite values.
Results may differ from the reference program's by a relative error of at most 0.0053.
Values may be sent and summed in bfloat16 or wider, within the bound.
A program may use at most 128 MiB of HBM per device.

```python
import math
import jax
import jax.numpy as jnp
from jax import lax

C = 1536
CH = 768
SEQS = 4
DILATION_BINS = 128
BINS = 2048


def raised(array, key, source, target, blocks, factor):
    owner, partner = [(jnp.arange(array.shape[axis_at]) // (array.shape[axis_at] // blocks)).reshape([-1 if axis == axis_at else 1 for axis in range(array.ndim)]) for axis_at in (source, target)]
    chosen = jax.random.permutation(key, blocks)[partner]
    strong = (owner == chosen) | (owner == (partner + blocks // 2) % blocks)
    return jnp.where(strong, factor * array, array)


def level_of(own_key, shape, cuts, smallest, largest):
    gain, own = 1.0, jax.random.fold_in(own_key, 6)
    for axis_at, blocks in cuts:
        draws = jnp.exp(jax.random.uniform(jax.random.fold_in(own, axis_at), (blocks,), jnp.float32, smallest / len(cuts), largest / len(cuts)))
        gain = gain * jnp.repeat(draws, shape[axis_at] // blocks).reshape([-1 if axis == axis_at else 1 for axis in range(len(shape))])
    return gain


def bell_draw(own_key, shape, width, reach, pieces=(), held_as=jnp.bfloat16):
    entries = width * jax.random.normal(own_key, shape, jnp.float32)
    if pieces:
        entries = entries * level_of(own_key, shape, pieces, -0.22, 0.18)
    return jnp.clip(entries, -reach, reach).astype(held_as)


def bell_draw_with(stream_key, dims, width, bound, pieces, heavy, kind=jnp.bfloat16):
    values = width * jax.random.normal(stream_key, dims, jnp.float32)
    if pieces:
        values = values * level_of(stream_key, dims, pieces, -0.22, 0.18)
    return jnp.clip(raised(values, jax.random.fold_in(stream_key, 3), *heavy), -bound, bound).astype(kind)


def setup_inputs(seed: int = 0) -> dict:
    streams_of = jax.random.split(jax.random.key(seed), 5)
    inputs = bell_draw(streams_of[0], (SEQS, BINS, C), 1.0, 6.0, ((1, 32),))
    cotangent = bell_draw_with(streams_of[1], (SEQS, BINS, C), 1.0, 6.0, ((1, 32),), (1, 2, 32, 2.75))
    dilated_kernel_weight = bell_draw(streams_of[2], (C, 3, CH), (3 * C) ** -0.5, 0.09375, ((0, 8), (2, 4)))
    point_weight = bell_draw(streams_of[3], (C, CH), CH ** -0.5, 0.21875, ((0, 8), (1, 4)))
    return dict(inputs=inputs, cotangent=cotangent, dilated_kernel_weight=dilated_kernel_weight, point_weight=point_weight)


def gelu_value(v):
    return 0.5 * v * (1.0 + lax.erf(v * (1.0 / math.sqrt(2.0))))

def gelu_slope(v):
    return 0.5 * (1.0 + lax.erf(v * (1.0 / math.sqrt(2.0)))) + v * jnp.exp(-0.5 * v * v) * (1.0 / math.sqrt(2.0 * math.pi))

def shifted_bin_rows(field, offset):
    zeros = jnp.zeros((field.shape[0], abs(offset), field.shape[2]), field.dtype)
    if offset > 0:
        return jnp.concatenate([zeros, field[:, :-offset]], axis=1)
    return jnp.concatenate([field[:, -offset:], zeros], axis=1)

def reference(inputs, cotangent, dilated_kernel_weight, point_weight):
    seqs, bins, kernel_width = inputs.shape
    half_kernel_span = point_weight.shape[1]
    x = inputs.astype(jnp.float32)
    scale = lax.rsqrt(lax.optimization_barrier(jnp.mean(x * x, axis=-1, keepdims=True)) + 1e-06)
    normed = x * scale
    input_activations = gelu_value(normed).astype(jnp.bfloat16)
    flat_acts = input_activations.reshape(-1, kernel_width)
    hidden_state = jnp.dot(shifted_bin_rows(input_activations, DILATION_BINS).reshape(-1, kernel_width), dilated_kernel_weight[:, 0, :], preferred_element_type=jnp.float32)
    hidden_state = hidden_state + jnp.dot(flat_acts, dilated_kernel_weight[:, 1, :], preferred_element_type=jnp.float32)
    hidden_state = hidden_state + jnp.dot(shifted_bin_rows(input_activations, -DILATION_BINS).reshape(-1, kernel_width), dilated_kernel_weight[:, 2, :], preferred_element_type=jnp.float32)
    mid = gelu_value(hidden_state).astype(jnp.bfloat16)
    mixed = jnp.dot(mid, point_weight.T, preferred_element_type=jnp.float32)
    outputs = (x.reshape(-1, kernel_width) + mixed).astype(jnp.bfloat16).reshape(seqs, bins, kernel_width)
    flat_cot = cotangent.reshape(-1, kernel_width)
    back_mid = jnp.dot(flat_cot, point_weight, preferred_element_type=jnp.float32)
    hidden_state_gradient = (back_mid * gelu_slope(hidden_state)).astype(jnp.bfloat16).reshape(seqs, bins, half_kernel_span)
    stacked_tap_inputs = jnp.concatenate([shifted_bin_rows(hidden_state_gradient, -DILATION_BINS), hidden_state_gradient, shifted_bin_rows(hidden_state_gradient, DILATION_BINS)], axis=-1).reshape(-1, 3 * half_kernel_span)
    norm_factor = 1.0 / math.sqrt(seqs * bins)
    grad_point = jnp.dot(flat_cot.T, mid, preferred_element_type=jnp.float32) * norm_factor
    grad_conv = jnp.dot(flat_acts.T, stacked_tap_inputs, preferred_element_type=jnp.float32).reshape(kernel_width, 3, half_kernel_span) * norm_factor
    grad_acts = jnp.dot(stacked_tap_inputs, dilated_kernel_weight.reshape(kernel_width, 3 * half_kernel_span).T, preferred_element_type=jnp.float32)
    grad_normed = grad_acts.reshape(seqs, bins, kernel_width) * gelu_slope(normed)
    inner = lax.optimization_barrier(jnp.mean(grad_normed * x, axis=-1, keepdims=True))
    grad_inputs = cotangent.astype(jnp.float32) + scale * (grad_normed - x * scale * scale * inner)
    return (outputs, grad_inputs.astype(jnp.bfloat16), grad_conv, grad_point)
```

```python
import functools
import math

import jax
import jax.numpy as jnp
from jax import lax
from jax.experimental import pallas as pl
from jax.experimental.pallas import tpu as pltpu
from jax.sharding import PartitionSpec as P

MESH = pl.DeviceIdType.MESH


def gelu_value(v):
    return 0.5 * v * (1.0 + lax.erf(v * (1.0 / math.sqrt(2.0))))


def gelu_slope(v):
    return 0.5 * (1.0 + lax.erf(v * (1.0 / math.sqrt(2.0)))) + v * jnp.exp(-0.5 * v * v) * (
        1.0 / math.sqrt(2.0 * math.pi)
    )


def shifted(x, axis, by):
    peers = lax.axis_size(axis)
    pairs = [(i, i + by) for i in range(peers) if 0 <= i + by < peers]
    return lax.ppermute(x, axis, pairs)


def place():
    s, f = lax.axis_index("seq"), lax.axis_index("fsdp")
    return s // 2, s % 2, f // 2, f % 2


def flip(x, y, c, first, second):
    fx = (1 - c) * first + c * second
    fy = c * first + (1 - c) * second
    return x + fx * (1 - 2 * x), y + fy * (1 - 2 * y)


def at(z, x, y, c):
    return (z * 2 + x, y * 2 + c)


def remote(src, dst, send, recv, device):
    return pltpu.make_async_remote_copy(
        src_ref=src, dst_ref=dst, send_sem=send, recv_sem=recv, device_id=device,
        device_id_type=MESH,
    )


def greet(n, z, x, y, c):
    barrier = pltpu.get_barrier_semaphore()
    peers = [at(z, 1 - x, y, c), at(z, x, 1 - y, c), at(z, x, y, 1 - c)]
    for peer in peers:
        pl.semaphore_signal(barrier, inc=1, device_id=peer, device_id_type=MESH)

    def hello(j, carry):
        pl.semaphore_signal(
            barrier, inc=1, device_id=at((z + j) % n, x, y, c), device_id_type=MESH
        )
        return carry

    lax.fori_loop(1, n, hello, 0)
    return barrier


def loop(lo, hi, f):
    def step(i, carry):
        f(i)
        return carry

    lax.fori_loop(lo, hi, step, 0)


def gather_kernel(n, shift, pack, acts, full, back, ahead, own_sem, zs, zr, as_, ar, bs, br, cs,
                  cr, hs, hr):
    z, x, y, c = place()
    linear = (z * 2 + x) * 4 + y * 2 + c
    total = n * 8
    barrier = greet(n, z, x, y, c)
    has_next = linear + shift < total
    has_prev = linear >= shift
    nxt = ((linear + shift) // 4, (linear + shift) % 4)
    prv = ((linear + total - shift) // 4 % (2 * n), (linear + total - shift) % 4)

    @pl.when(has_next)
    def _():
        pl.semaphore_signal(barrier, inc=1, device_id=nxt, device_id_type=MESH)

    @pl.when(has_prev)
    def _():
        pl.semaphore_signal(barrier, inc=1, device_id=prv, device_id_type=MESH)

    near = 2 - (linear + shift) // total - (total - 1 - linear + shift) // total
    pl.semaphore_wait(barrier, 3 + n - 1 + near)

    def spot(zz, xx, yy, cc):
        return full.at[yy * 2 + cc, zz * 2 + xx]

    x1, y1 = flip(x, y, c, 1, 0)
    x2, y2 = flip(x, y, c, 0, 1)
    to_a, to_b, to_c = at(z, x1, y1, c), at(z, x2, y2, c), at(z, x, y, 1 - c)
    own = spot(z, x, y, c)
    keep = pltpu.make_async_copy(pack, own, own_sem)
    keep.start()

    def send_z(j):
        remote(pack, own, zs.at[j], zr.at[j], at((z + j) % n, x, y, c)).start()

    def send_abc(j, src, dst):
        remote(src, dst, as_.at[j], ar.at[j], to_a).start()
        remote(src, dst, bs.at[j], br.at[j], to_b).start()
        remote(src, dst, cs.at[j], cr.at[j], to_c).start()

    loop(1, n, send_z)
    send_abc(0, pack, own)

    @pl.when(has_next)
    def _():
        remote(acts, back, hs.at[0], hr.at[0], nxt).start()

    @pl.when(has_prev)
    def _():
        remote(acts, ahead, hs.at[1], hr.at[1], prv).start()

    def zof(j):
        return (z + n - j) % n

    def step_z(j):
        b = spot(zof(j), x, y, c)
        remote(b, b, zs.at[j], zr.at[j], to_a).wait_recv()
        send_abc(j, b, b)

    loop(1, n, step_z)

    def step_a(j):
        b = spot(zof(j), x1, y1, c)
        remote(b, b, as_.at[j], ar.at[j], to_a).wait_recv()
        remote(b, b, bs.at[n + j], br.at[n + j], to_b).start()
        remote(b, b, cs.at[n + j], cr.at[n + j], to_c).start()

    loop(0, n, step_a)

    def step_b(m):
        fx, fy = flip(x, y, c, m // n, 1)
        b = spot(zof(m % n), fx, fy, c)
        remote(b, b, bs.at[m], br.at[m], to_b).wait_recv()
        remote(b, b, cs.at[2 * n + m], cr.at[2 * n + m], to_c).start()

    loop(0, 2 * n, step_b)

    def step_c(m):
        q = m // n
        fx, fy = flip(x, y, 1 - c, q % 2, q // 2)
        b = spot(zof(m % n), fx, fy, 1 - c)
        remote(b, b, cs.at[m], cr.at[m], to_c).wait_recv()

    loop(0, 4 * n, step_c)

    def sent(sems, recv):
        def f(j):
            remote(pack, own, sems.at[j], recv.at[j], to_a).wait_send()

        return f

    loop(1, n, sent(zs, zr))
    loop(0, n, sent(as_, ar))
    loop(0, 2 * n, sent(bs, br))
    loop(0, 4 * n, sent(cs, cr))
    keep.wait()

    @pl.when(has_next)
    def _():
        remote(acts, ahead, hs.at[0], hr.at[1], nxt).wait()

    @pl.when(has_prev)
    def _():
        remote(acts, back, hs.at[1], hr.at[0], prv).wait()


def reduce_kernel(n, norm, left, right, out, sa, ka, ra, rb, rc, rd, as_, ar, bs, br, cs, cr,
                  ds, dr):
    z, x, y, c = place()
    barrier = greet(n, z, x, y, c)
    x1, y1 = flip(x, y, c, 1, 0)
    x2, y2 = flip(x, y, c, 0, 1)
    to_c, to_b, to_a = at(z, x1, y1, c), at(z, x2, y2, c), at(z, x, y, 1 - c)

    def zof(t):
        return (z + t + 1) % n

    def block(m, core):
        q = m // n
        fx, fy = flip(x, y, core, 1 - q % 2, 1 - q // 2)
        s, f = at(zof(m % n), fx, fy, core)
        return jnp.dot(left[s], right[f], preferred_element_type=jnp.float32)

    sa[0] = block(0, 1 - c).astype(sa.dtype)
    pl.semaphore_wait(barrier, 3 + n - 1)

    def copy_a(m):
        return remote(sa.at[m], ra.at[m], as_.at[m], ar.at[m], to_a)

    def copy_b(m):
        return remote(ra.at[m], rb.at[m], bs.at[m], br.at[m], to_b)

    def copy_c(j):
        return remote(ra.at[2 * n + j], rc.at[j], cs.at[j], cr.at[j], to_c)

    def copy_d(t):
        return remote(ra.at[3 * n + t], rd.at[t], ds.at[t], dr.at[t], at(zof(t), x, y, c))

    copy_a(0).start()

    def step_send(m):
        sa[m] = block(m, 1 - c).astype(sa.dtype)
        copy_a(m).start()

    loop(1, 4 * n, step_send)

    def step_b(m):
        mine = block(m, c)
        copy_a(m).wait_recv()
        ra[m] = (ra[m].astype(jnp.float32) + mine).astype(ra.dtype)
        copy_b(m).start()

    loop(0, 2 * n, step_b)

    def step_k(m):
        ka[m] = block(2 * n + m, c).astype(ka.dtype)

    loop(0, 2 * n, step_k)

    def three(m):
        copy_a(2 * n + m).wait_recv()
        copy_b(m).wait_recv()
        return (
            ra[2 * n + m].astype(jnp.float32)
            + ka[m].astype(jnp.float32)
            + rb[m].astype(jnp.float32)
        )

    def step_c(j):
        ra[2 * n + j] = three(j).astype(ra.dtype)
        copy_c(j).start()

    loop(0, n, step_c)

    def step_d(t):
        part = three(n + t)
        copy_c(t).wait_recv()
        ra[3 * n + t] = (part + rc[t].astype(jnp.float32)).astype(ra.dtype)
        copy_d(t).start()

    loop(0, n - 1, step_d)
    part = three(2 * n - 1)
    copy_c(n - 1).wait_recv()
    out[...] = part + rc[n - 1].astype(jnp.float32)

    def step_out(t):
        copy_d(t).wait_recv()
        out[...] += rd[t].astype(jnp.float32)

    loop(0, n - 1, step_out)
    out[...] = out[...] * norm
    loop(0, 4 * n, lambda m: copy_a(m).wait_send())
    loop(0, 2 * n, lambda m: copy_b(m).wait_send())
    loop(0, n, lambda m: copy_c(m).wait_send())
    loop(0, n - 1, lambda m: copy_d(m).wait_send())


def body(inputs, cotangent, dilated_kernel_weight, point_weight):
    seqs, bins, width = inputs.shape
    peers, cols = lax.axis_size("seq"), lax.axis_size("fsdp")
    n = peers // 2
    shift = 128 // bins
    rows = seqs * bins
    norm_factor = 1.0 / math.sqrt(rows * peers * cols)
    wr, _, wc = dilated_kernel_weight.shape
    bf, f32 = jnp.bfloat16, jnp.float32
    pack = jnp.concatenate(
        [dilated_kernel_weight[:, 0], dilated_kernel_weight[:, 1], dilated_kernel_weight[:, 2],
         point_weight], axis=1)
    x = inputs.astype(f32).reshape(rows, width)
    cot = cotangent.reshape(rows, width)
    scale = lax.rsqrt(jnp.mean(x * x, axis=-1, keepdims=True) + 1e-06)
    normed = x * scale
    acts = gelu_value(normed).astype(bf)
    sem = pltpu.SemaphoreType.DMA
    anyspec = pl.BlockSpec(memory_space=pl.ANY)
    vspec = pl.BlockSpec(memory_space=pltpu.VMEM)
    full, back, ahead = pl.pallas_call(
        functools.partial(gather_kernel, n, shift),
        out_shape=(
            jax.ShapeDtypeStruct((cols, peers, wr, 4 * wc), bf),
            jax.ShapeDtypeStruct((rows, width), bf),
            jax.ShapeDtypeStruct((rows, width), bf),
        ),
        in_specs=[anyspec, anyspec],
        out_specs=[anyspec, anyspec, anyspec],
        scratch_shapes=[sem(()), sem((n,)), sem((n,)), sem((n,)), sem((n,)), sem((2 * n,)),
                        sem((2 * n,)), sem((4 * n,)), sem((4 * n,)), sem((2,)), sem((2,))],
        compiler_params=pltpu.CompilerParams(collective_id=0, has_side_effects=True),
    )(pack, acts)
    linear = lax.axis_index("seq") * cols + lax.axis_index("fsdp")
    back = jnp.where(linear >= shift, back, jnp.zeros((), bf))
    ahead = jnp.where(linear + shift < peers * cols, ahead, jnp.zeros((), bf))
    full = full.reshape(cols, width, 4 * wc)
    stacked = jnp.concatenate([back, acts, ahead, cot], axis=0)
    prod = [jnp.dot(stacked, full[f], preferred_element_type=f32) for f in range(cols)]
    hidden = jnp.stack([
        p[:rows, :wc] + p[rows:2 * rows, wc:2 * wc] + p[2 * rows:3 * rows, 2 * wc:3 * wc]
        for p in prod])
    back_mid = jnp.stack([p[3 * rows:, 3 * wc:] for p in prod])
    mid = gelu_value(hidden).astype(bf)
    grad = (back_mid * gelu_slope(hidden)).astype(bf)
    later = shifted(grad, ("seq", "fsdp"), -shift)
    earlier = shifted(grad, ("seq", "fsdp"), shift)
    none = jnp.zeros_like(grad)
    right = jnp.concatenate([
        jnp.concatenate([later, grad, earlier, none], axis=2),
        jnp.concatenate([none, none, none, mid], axis=2)], axis=1)
    left = jnp.concatenate([acts, cot], axis=0).T.reshape(peers, wr, 2 * rows)
    slot = lambda k: pltpu.VMEM((k, wr, 4 * wc), bf)
    reduced = pl.pallas_call(
        functools.partial(reduce_kernel, n, norm_factor),
        out_shape=jax.ShapeDtypeStruct((wr, 4 * wc), f32),
        in_specs=[vspec, vspec],
        out_specs=vspec,
        scratch_shapes=[slot(4 * n), slot(2 * n), slot(4 * n), slot(2 * n), slot(n), slot(n - 1),
                        sem((4 * n,)), sem((4 * n,)), sem((2 * n,)), sem((2 * n,)), sem((n,)),
                        sem((n,)), sem((n - 1,)), sem((n - 1,))],
        compiler_params=pltpu.CompilerParams(
            collective_id=1, has_side_effects=True, vmem_limit_bytes=52 * 1024 * 1024),
    )(left, right)
    both = sum(
        lax.dot_general(right[f], full[f], (((1,), (1,)), ((), ())), preferred_element_type=f32)
        for f in range(cols))
    outputs = (x + both[rows:]).astype(bf).reshape(seqs, bins, width)
    grad_normed = both[:rows] * gelu_slope(normed)
    inner = jnp.mean(grad_normed * x, axis=-1, keepdims=True)
    grad_inputs = (
        cot.astype(f32) + scale * (grad_normed - x * scale * scale * inner)
    ).astype(bf).reshape(seqs, bins, width)
    grad_conv = reduced[:, :3 * wc].reshape(wr, 3, wc)
    grad_point = reduced[:, 3 * wc:]
    return (outputs, grad_inputs, grad_conv, grad_point)


def solution(mesh):
    specs = (
        P(None, ("seq", "fsdp"), None),
        P(None, ("seq", "fsdp"), None),
        P("seq", None, "fsdp"),
        P("seq", "fsdp"),
    )
    return jax.shard_map(body, mesh=mesh, in_specs=specs, out_specs=specs, check_vma=False)
```

```python
import functools
import math

import jax
import jax.numpy as jnp
from jax import lax
from jax.experimental import pallas as pl
from jax.experimental.pallas import tpu as pltpu
from jax.sharding import PartitionSpec as P

MESH = pl.DeviceIdType.MESH


def gelu_value(v):
    return 0.5 * v * (1.0 + lax.erf(v * (1.0 / math.sqrt(2.0))))


def gelu_slope(v):
    return 0.5 * (1.0 + lax.erf(v * (1.0 / math.sqrt(2.0)))) + v * jnp.exp(-0.5 * v * v) * (
        1.0 / math.sqrt(2.0 * math.pi)
    )


def place():
    s, f = lax.axis_index("seq"), lax.axis_index("fsdp")
    return s // 2, s % 2, f // 2, f % 2


def flip(x, y, c, first, second):
    fx = (1 - c) * first + c * second
    fy = c * first + (1 - c) * second
    return x + fx * (1 - 2 * x), y + fy * (1 - 2 * y)


def at(z, x, y, c):
    return (z * 2 + x, y * 2 + c)


def remote(src, dst, send, recv, device):
    return pltpu.make_async_remote_copy(
        src_ref=src, dst_ref=dst, send_sem=send, recv_sem=recv, device_id=device,
        device_id_type=MESH,
    )


def greet(n, z, x, y, c):
    barrier = pltpu.get_barrier_semaphore()
    peers = [at(z, 1 - x, y, c), at(z, x, 1 - y, c), at(z, x, y, 1 - c)]
    for peer in peers:
        pl.semaphore_signal(barrier, inc=1, device_id=peer, device_id_type=MESH)

    def hello(j, carry):
        pl.semaphore_signal(
            barrier, inc=1, device_id=at((z + j) % n, x, y, c), device_id_type=MESH
        )
        return carry

    lax.fori_loop(1, n, hello, 0)
    return barrier


def loop(lo, hi, f):
    def step(i, carry):
        f(i)
        return carry

    lax.fori_loop(lo, hi, step, 0)


def line(n, shift, z, x, y, c):
    linear, total = (z * 2 + x) * 4 + y * 2 + c, n * 8
    has_next, has_prev = linear + shift < total, linear >= shift
    up, down = (linear + shift) % total, (linear + total - shift) % total
    near = 2 - (linear + shift) // total - (total - 1 - linear + shift) // total
    return has_next, has_prev, (up // 4, up % 4), (down // 4, down % 4), near


def greet_line(barrier, has_next, has_prev, nxt, prv):
    @pl.when(has_next)
    def _():
        pl.semaphore_signal(barrier, inc=1, device_id=nxt, device_id_type=MESH)

    @pl.when(has_prev)
    def _():
        pl.semaphore_signal(barrier, inc=1, device_id=prv, device_id_type=MESH)


def halo_start(has_next, has_prev, nxt, prv, up, down, from_prev, from_next, hs, hr):
    @pl.when(has_next)
    def _():
        remote(up, from_prev, hs.at[0], hr.at[0], nxt).start()

    @pl.when(has_prev)
    def _():
        remote(down, from_next, hs.at[1], hr.at[1], prv).start()


def halo_wait(has_next, has_prev, nxt, prv, up, down, from_prev, from_next, hs, hr):
    @pl.when(has_next)
    def _():
        remote(up, from_next, hs.at[0], hr.at[1], nxt).wait()

    @pl.when(has_prev)
    def _():
        remote(down, from_prev, hs.at[1], hr.at[0], prv).wait()

    @pl.when(jnp.logical_not(has_next))
    def _():
        from_next[...] = jnp.zeros_like(from_next)

    @pl.when(jnp.logical_not(has_prev))
    def _():
        from_prev[...] = jnp.zeros_like(from_prev)


def gather_kernel(n, shift, pack0, pack1, acts, full0, full1, back, ahead, up, down, own_sem, zs,
                  zr, as_, ar, bs, br, cs, cr, hs, hr):
    z, x, y, c = place()
    barrier = greet(n, z, x, y, c)
    has_next, has_prev, nxt, prv, near = line(n, shift, z, x, y, c)
    greet_line(barrier, has_next, has_prev, nxt, prv)
    pl.semaphore_wait(barrier, 3 + n - 1 + near)
    packs, fulls = (pack0, pack1), (full0, full1)

    def spot(h, zz, xx, yy, cc):
        return fulls[h].at[yy * 2 + cc, zz * 2 + xx]

    x1, y1 = flip(x, y, c, 1, 0)
    x2, y2 = flip(x, y, c, 0, 1)
    to_a, to_b, to_c = at(z, x1, y1, c), at(z, x2, y2, c), at(z, x, y, 1 - c)

    def zof(j):
        return (z + n - j) % n

    def copy_z(h, j):
        return remote(packs[h], spot(h, z, x, y, c), zs.at[h, j], zr.at[h, j],
                      at((z + j) % n, x, y, c))

    def copy_a(h, j, src, dst):
        return remote(src, dst, as_.at[h, j], ar.at[h, j], to_a)

    def copy_b(h, j, src, dst):
        return remote(src, dst, bs.at[h, j], br.at[h, j], to_b)

    def copy_c(h, j, src, dst):
        return remote(src, dst, cs.at[h, j], cr.at[h, j], to_c)

    def keep(h):
        return pltpu.make_async_copy(packs[h], spot(h, z, x, y, c), own_sem.at[h])

    def send_abc(h, j, src, dst):
        copy_a(h, j, src, dst).start()
        copy_b(h, j, src, dst).start()
        copy_c(h, j, src, dst).start()

    def own(h):
        loop(1, n, lambda j: copy_z(h, j).start())
        send_abc(h, 0, packs[h], spot(h, z, x, y, c))
        keep(h).start()

    def steps_z(h):
        def f(j):
            b = spot(h, zof(j), x, y, c)
            remote(b, b, zs.at[h, j], zr.at[h, j], to_a).wait_recv()
            send_abc(h, j, b, b)

        loop(1, n, f)

    def steps_a(h):
        def f(j):
            b = spot(h, zof(j), x1, y1, c)
            copy_a(h, j, b, b).wait_recv()
            copy_b(h, n + j, b, b).start()
            copy_c(h, n + j, b, b).start()

        loop(0, n, f)

    def steps_b(h):
        def f(m):
            fx, fy = flip(x, y, c, m // n, 1)
            b = spot(h, zof(m % n), fx, fy, c)
            copy_b(h, m, b, b).wait_recv()
            copy_c(h, 2 * n + m, b, b).start()

        loop(0, 2 * n, f)

    def steps_c(h):
        def f(m):
            q = m // n
            fx, fy = flip(x, y, 1 - c, q % 2, q // 2)
            b = spot(h, zof(m % n), fx, fy, 1 - c)
            copy_c(h, m, b, b).wait_recv()

        loop(0, 4 * n, f)

    def sent(h):
        b = spot(h, z, x, y, c)
        loop(1, n, lambda j: copy_z(h, j).wait_send())
        loop(0, n, lambda j: copy_a(h, j, b, b).wait_send())
        loop(0, 2 * n, lambda j: copy_b(h, j, b, b).wait_send())
        loop(0, 4 * n, lambda j: copy_c(h, j, b, b).wait_send())

    own(0)
    own(1)
    steps_z(0)
    steps_a(0)
    steps_b(0)
    steps_z(1)
    steps_c(0)
    keep(0).wait()
    rows, wc = acts.shape[1], pack0.shape[1] // 2
    parts = []
    for f in range(4):
        def add(s, total, f=f):
            return total + jnp.dot(acts[s], full0[f, s], preferred_element_type=jnp.float32)

        part = lax.fori_loop(0, 2 * n, add, jnp.zeros((rows, 2 * wc), jnp.float32))
        parts.append(part.astype(up.dtype))
    up[...] = jnp.concatenate([p[:, :wc] for p in parts], axis=1)
    down[...] = jnp.concatenate([p[:, wc:] for p in parts], axis=1)
    halo = (has_next, has_prev, nxt, prv, up, down, back, ahead, hs, hr)
    halo_start(*halo)
    steps_a(1)
    steps_b(1)
    steps_c(1)
    keep(1).wait()
    halo_wait(*halo)
    sent(0)
    sent(1)


def reduce_kernel(n, shift, norm, left, right, grad, out, edge, sa, ra, rb, rc, rd, later,
                  earlier, as_, ar, bs, br, cs, cr, ds, dr, hs, hr):
    z, x, y, c = place()
    barrier = greet(n, z, x, y, c)
    has_next, has_prev, nxt, prv, near = line(n, shift, z, x, y, c)
    greet_line(barrier, has_next, has_prev, nxt, prv)
    rows, wc2 = edge.shape[1:]
    wc = wc2 // 2
    x1, y1 = flip(x, y, c, 1, 0)
    x2, y2 = flip(x, y, c, 0, 1)
    to_c, to_b, to_a = at(z, x1, y1, c), at(z, x2, y2, c), at(z, x, y, 1 - c)

    def zof(t):
        return (z + t + 1) % n

    def block(h, m, core):
        q = m // n
        fx, fy = flip(x, y, core, 1 - q % 2, 1 - q // 2)
        s, f = at(zof(m % n), fx, fy, core)
        if h == 0:
            return jnp.dot(left[s], right[f], preferred_element_type=jnp.float32)
        return jnp.dot(left[s, :, :rows], edge[f], preferred_element_type=jnp.float32)

    sa[0, 0] = block(0, 0, 1 - c).astype(sa.dtype)
    pl.semaphore_wait(barrier, 3 + n - 1 + near)
    halo = (has_next, has_prev, nxt, prv, grad, grad, earlier, later, hs, hr)

    def copy_a(h, m):
        return remote(sa.at[h, m], ra.at[h, m], as_.at[h, m], ar.at[h, m], to_a)

    def copy_b(h, m):
        return remote(ra.at[h, m], rb.at[h, m], bs.at[h, m], br.at[h, m], to_b)

    def copy_c(h, j):
        return remote(ra.at[h, 2 * n + j], rc.at[h, j], cs.at[h, j], cr.at[h, j], to_c)

    def copy_d(h, t):
        return remote(ra.at[h, 3 * n + t], rd.at[h, t], ds.at[h, t], dr.at[h, t],
                      at(zof(t), x, y, c))

    def sends(h, first):
        def f(m):
            sa[h, m] = block(h, m, 1 - c).astype(sa.dtype)
            copy_a(h, m).start()

        loop(first, 4 * n, f)

    def steps_b(h):
        def f(m):
            mine = block(h, m, c)
            copy_a(h, m).wait_recv()
            ra[h, m] = (ra[h, m].astype(jnp.float32) + mine).astype(ra.dtype)
            copy_b(h, m).start()

        loop(0, 2 * n, f)

    def three(h, m):
        mine = block(h, 2 * n + m, c)
        copy_a(h, 2 * n + m).wait_recv()
        copy_b(h, m).wait_recv()
        return ra[h, 2 * n + m].astype(jnp.float32) + mine + rb[h, m].astype(jnp.float32)

    def steps_c(h):
        def f(j):
            ra[h, 2 * n + j] = three(h, j).astype(ra.dtype)
            copy_c(h, j).start()

        loop(0, n, f)

    def steps_d(h):
        def f(t):
            part = three(h, n + t)
            copy_c(h, t).wait_recv()
            ra[h, 3 * n + t] = (part + rc[h, t].astype(jnp.float32)).astype(ra.dtype)
            copy_d(h, t).start()

        loop(0, n - 1, f)
        part = three(h, 2 * n - 1)
        copy_c(h, n - 1).wait_recv()
        out[h] = part + rc[h, n - 1].astype(jnp.float32)

    def steps_out(h):
        def f(t):
            copy_d(h, t).wait_recv()
            out[h] += rd[h, t].astype(jnp.float32)

        loop(0, n - 1, f)
        out[h] = out[h] * norm

    copy_a(0, 0).start()
    halo_start(*halo)
    sends(0, 1)
    steps_b(0)
    halo_wait(*halo)
    for f in range(4):
        cols = slice(f * wc, (f + 1) * wc)
        edge[f] = jnp.concatenate([later[:, cols], earlier[:, cols]], axis=1)
    sends(1, 0)
    steps_b(1)
    steps_c(0)
    steps_c(1)
    steps_d(0)
    steps_d(1)
    steps_out(0)
    steps_out(1)
    for h in range(2):
        loop(0, 4 * n, lambda m: copy_a(h, m).wait_send())
        loop(0, 2 * n, lambda m: copy_b(h, m).wait_send())
        loop(0, n, lambda m: copy_c(h, m).wait_send())
        loop(0, n - 1, lambda m: copy_d(h, m).wait_send())


def body(inputs, cotangent, dilated_kernel_weight, point_weight):
    seqs, bins, width = inputs.shape
    peers, cols = lax.axis_size("seq"), lax.axis_size("fsdp")
    n = peers // 2
    shift = 128 // bins
    rows = seqs * bins
    norm_factor = 1.0 / math.sqrt(rows * peers * cols)
    wr, _, wc = dilated_kernel_weight.shape
    span = cols * wc
    bf, f32 = jnp.bfloat16, jnp.float32
    pack0 = jnp.concatenate([dilated_kernel_weight[:, 0], dilated_kernel_weight[:, 2]], axis=1)
    pack1 = jnp.concatenate([dilated_kernel_weight[:, 1], point_weight], axis=1)
    x = inputs.astype(f32).reshape(rows, width)
    cot = cotangent.reshape(rows, width)
    scale = lax.rsqrt(jnp.mean(x * x, axis=-1, keepdims=True) + 1e-06)
    normed = x * scale
    acts = gelu_value(normed).astype(bf)
    split = acts.reshape(rows, peers, wr).transpose(1, 0, 2)
    sem = lambda *k: pltpu.SemaphoreType.DMA(k)
    anyspec = pl.BlockSpec(memory_space=pl.ANY)
    vspec = pl.BlockSpec(memory_space=pltpu.VMEM)
    half = jax.ShapeDtypeStruct((cols, peers, wr, 2 * wc), bf)
    halo = jax.ShapeDtypeStruct((rows, span), bf)
    full0, full1, back, ahead = pl.pallas_call(
        functools.partial(gather_kernel, n, shift),
        out_shape=(half, half, halo, halo),
        in_specs=[anyspec, anyspec, vspec],
        out_specs=[vspec, anyspec, vspec, vspec],
        scratch_shapes=[pltpu.VMEM((rows, span), bf), pltpu.VMEM((rows, span), bf),
                        sem(2), sem(2, n), sem(2, n), sem(2, n), sem(2, n), sem(2, 2 * n),
                        sem(2, 2 * n), sem(2, 4 * n), sem(2, 4 * n), sem(2), sem(2)],
        compiler_params=pltpu.CompilerParams(
            collective_id=0, has_side_effects=True, vmem_limit_bytes=40 * 1024 * 1024),
    )(pack0, pack1, split)
    full0 = full0.reshape(cols, width, 2 * wc)
    full1 = full1.reshape(cols, width, 2 * wc)
    stacked = jnp.concatenate([acts, cot], axis=0)
    prod = [jnp.dot(stacked, full1[f], preferred_element_type=f32) for f in range(cols)]
    hidden = (jnp.concatenate([p[:rows, :wc] for p in prod], axis=1)
              + back.astype(f32) + ahead.astype(f32))
    back_mid = jnp.concatenate([p[rows:, wc:] for p in prod], axis=1)
    mid = gelu_value(hidden).astype(bf)
    grad = (back_mid * gelu_slope(hidden)).astype(bf)
    none = jnp.zeros((rows, wc), bf)
    right = jnp.stack([
        jnp.concatenate([
            jnp.concatenate([grad[:, f * wc:(f + 1) * wc], none], axis=1),
            jnp.concatenate([none, mid[:, f * wc:(f + 1) * wc]], axis=1)], axis=0)
        for f in range(cols)])
    left = stacked.T.reshape(peers, wr, 2 * rows)
    slot = lambda k: pltpu.VMEM((2, k, wr, 2 * wc), bf)
    reduced, edge = pl.pallas_call(
        functools.partial(reduce_kernel, n, shift, norm_factor),
        out_shape=(jax.ShapeDtypeStruct((2, wr, 2 * wc), f32),
                   jax.ShapeDtypeStruct((cols, rows, 2 * wc), bf)),
        in_specs=[vspec, vspec, vspec],
        out_specs=[vspec, vspec],
        scratch_shapes=[slot(4 * n), slot(4 * n), slot(2 * n), slot(n), slot(n - 1),
                        pltpu.VMEM((rows, span), bf), pltpu.VMEM((rows, span), bf),
                        sem(2, 4 * n), sem(2, 4 * n), sem(2, 2 * n), sem(2, 2 * n), sem(2, n),
                        sem(2, n), sem(2, n - 1), sem(2, n - 1), sem(2), sem(2)],
        compiler_params=pltpu.CompilerParams(
            collective_id=1, has_side_effects=True, vmem_limit_bytes=52 * 1024 * 1024),
    )(left, right, grad)
    against = (((1,), (1,)), ((), ()))
    both = sum(
        lax.dot_general(right[f], full1[f], against, preferred_element_type=f32)
        for f in range(cols))
    sides = sum(
        lax.dot_general(edge[f], full0[f], against, preferred_element_type=f32)
        for f in range(cols))
    outputs = (x + both[rows:]).astype(bf).reshape(seqs, bins, width)
    grad_normed = (both[:rows] + sides) * gelu_slope(normed)
    inner = jnp.mean(grad_normed * x, axis=-1, keepdims=True)
    grad_inputs = (
        cot.astype(f32) + scale * (grad_normed - x * scale * scale * inner)
    ).astype(bf).reshape(seqs, bins, width)
    grad_conv = jnp.stack([reduced[1, :, :wc], reduced[0, :, :wc], reduced[1, :, wc:]], axis=1)
    grad_point = reduced[0, :, wc:]
    return (outputs, grad_inputs, grad_conv, grad_point)


def solution(mesh):
    specs = (
        P(None, ("seq", "fsdp"), None),
        P(None, ("seq", "fsdp"), None),
        P("seq", None, "fsdp"),
        P("seq", "fsdp"),
    )
    return jax.shard_map(body, mesh=mesh, in_specs=specs, out_specs=specs, check_vma=False)
```

```python
import functools
import math

import jax
import jax.numpy as jnp
from jax import lax
from jax.experimental import pallas as pl
from jax.experimental.pallas import tpu as pltpu
from jax.sharding import PartitionSpec as P

MESH = pl.DeviceIdType.MESH


def gelu_value(v):
    return 0.5 * v * (1.0 + lax.erf(v * (1.0 / math.sqrt(2.0))))


def gelu_slope(v):
    return 0.5 * (1.0 + lax.erf(v * (1.0 / math.sqrt(2.0)))) + v * jnp.exp(-0.5 * v * v) * (
        1.0 / math.sqrt(2.0 * math.pi)
    )


def place():
    s, f = lax.axis_index("seq"), lax.axis_index("fsdp")
    return s // 2, s % 2, f // 2, f % 2


def flip(x, y, c, first, second):
    fx = (1 - c) * first + c * second
    fy = c * first + (1 - c) * second
    return x + fx * (1 - 2 * x), y + fy * (1 - 2 * y)


def at(z, x, y, c):
    return (z * 2 + x, y * 2 + c)


def remote(src, dst, send, recv, device):
    return pltpu.make_async_remote_copy(
        src_ref=src, dst_ref=dst, send_sem=send, recv_sem=recv, device_id=device,
        device_id_type=MESH,
    )


def greet(n, z, x, y, c):
    barrier = pltpu.get_barrier_semaphore()
    peers = [at(z, 1 - x, y, c), at(z, x, 1 - y, c), at(z, x, y, 1 - c)]
    for peer in peers:
        pl.semaphore_signal(barrier, inc=1, device_id=peer, device_id_type=MESH)

    def hello(j, carry):
        pl.semaphore_signal(
            barrier, inc=1, device_id=at((z + j) % n, x, y, c), device_id_type=MESH
        )
        return carry

    lax.fori_loop(1, n, hello, 0)
    return barrier


def loop(lo, hi, f):
    def step(i, carry):
        f(i)
        return carry

    lax.fori_loop(lo, hi, step, 0)


def line(n, shift, z, x, y, c):
    linear, total = (z * 2 + x) * 4 + y * 2 + c, n * 8
    has_next, has_prev = linear + shift < total, linear >= shift
    up, down = (linear + shift) % total, (linear + total - shift) % total
    near = 2 - (linear + shift) // total - (total - 1 - linear + shift) // total
    return has_next, has_prev, (up // 4, up % 4), (down // 4, down % 4), near


def greet_line(barrier, has_next, has_prev, nxt, prv):
    @pl.when(has_next)
    def _():
        pl.semaphore_signal(barrier, inc=1, device_id=nxt, device_id_type=MESH)

    @pl.when(has_prev)
    def _():
        pl.semaphore_signal(barrier, inc=1, device_id=prv, device_id_type=MESH)


def halo_start(has_next, has_prev, nxt, prv, up, down, from_prev, from_next, hs, hr):
    @pl.when(has_next)
    def _():
        remote(up, from_prev, hs.at[0], hr.at[0], nxt).start()

    @pl.when(has_prev)
    def _():
        remote(down, from_next, hs.at[1], hr.at[1], prv).start()


def halo_wait(has_next, has_prev, nxt, prv, up, down, from_prev, from_next, hs, hr):
    @pl.when(has_next)
    def _():
        remote(up, from_next, hs.at[0], hr.at[1], nxt).wait()

    @pl.when(has_prev)
    def _():
        remote(down, from_prev, hs.at[1], hr.at[0], prv).wait()

    @pl.when(jnp.logical_not(has_next))
    def _():
        from_next[...] = jnp.zeros_like(from_next)

    @pl.when(jnp.logical_not(has_prev))
    def _():
        from_prev[...] = jnp.zeros_like(from_prev)


def gather_kernel(n, shift, pack0, pack1, acts, full0, full1, back, ahead, up, down, own_sem, zs,
                  zr, as_, ar, bs, br, cs, cr, hs, hr):
    z, x, y, c = place()
    barrier = greet(n, z, x, y, c)
    has_next, has_prev, nxt, prv, near = line(n, shift, z, x, y, c)
    greet_line(barrier, has_next, has_prev, nxt, prv)
    pl.semaphore_wait(barrier, 3 + n - 1 + near)
    packs, fulls = (pack0, pack1), (full0, full1)

    def spot(h, zz, xx, yy, cc):
        return fulls[h].at[yy * 2 + cc, zz * 2 + xx]

    x1, y1 = flip(x, y, c, 1, 0)
    x2, y2 = flip(x, y, c, 0, 1)
    to_a, to_b, to_c = at(z, x1, y1, c), at(z, x2, y2, c), at(z, x, y, 1 - c)

    def zof(j):
        return (z + n - j) % n

    def copy_z(h, j):
        return remote(packs[h], spot(h, z, x, y, c), zs.at[h, j], zr.at[h, j],
                      at((z + j) % n, x, y, c))

    def copy_a(h, j, src, dst):
        return remote(src, dst, as_.at[h, j], ar.at[h, j], to_a)

    def copy_b(h, j, src, dst):
        return remote(src, dst, bs.at[h, j], br.at[h, j], to_b)

    def copy_c(h, j, src, dst):
        return remote(src, dst, cs.at[h, j], cr.at[h, j], to_c)

    def keep(h):
        return pltpu.make_async_copy(packs[h], spot(h, z, x, y, c), own_sem.at[h])

    def send_abc(h, j, src, dst):
        copy_a(h, j, src, dst).start()
        copy_b(h, j, src, dst).start()
        copy_c(h, j, src, dst).start()

    def own(h):
        loop(1, n, lambda j: copy_z(h, j).start())
        send_abc(h, 0, packs[h], spot(h, z, x, y, c))
        keep(h).start()

    def steps_z(h):
        def f(j):
            b = spot(h, zof(j), x, y, c)
            remote(b, b, zs.at[h, j], zr.at[h, j], to_a).wait_recv()
            send_abc(h, j, b, b)

        loop(1, n, f)

    def steps_a(h):
        def f(j):
            b = spot(h, zof(j), x1, y1, c)
            copy_a(h, j, b, b).wait_recv()
            copy_b(h, n + j, b, b).start()
            copy_c(h, n + j, b, b).start()

        loop(0, n, f)

    def steps_b(h):
        def f(m):
            fx, fy = flip(x, y, c, m // n, 1)
            b = spot(h, zof(m % n), fx, fy, c)
            copy_b(h, m, b, b).wait_recv()
            copy_c(h, 2 * n + m, b, b).start()

        loop(0, 2 * n, f)

    def steps_c(h):
        def f(m):
            q = m // n
            fx, fy = flip(x, y, 1 - c, q % 2, q // 2)
            b = spot(h, zof(m % n), fx, fy, 1 - c)
            copy_c(h, m, b, b).wait_recv()

        loop(0, 4 * n, f)

    def sent(h):
        b = spot(h, z, x, y, c)
        loop(1, n, lambda j: copy_z(h, j).wait_send())
        loop(0, n, lambda j: copy_a(h, j, b, b).wait_send())
        loop(0, 2 * n, lambda j: copy_b(h, j, b, b).wait_send())
        loop(0, 4 * n, lambda j: copy_c(h, j, b, b).wait_send())

    own(0)
    own(1)
    steps_z(0)
    steps_a(0)
    steps_z(1)
    steps_b(0)
    steps_a(1)
    steps_c(0)
    keep(0).wait()
    rows, wc = acts.shape[1], pack0.shape[1] // 2
    parts = []
    for f in range(4):
        def add(s, total, f=f):
            return total + jnp.dot(acts[s], full0[f, s], preferred_element_type=jnp.float32)

        part = lax.fori_loop(0, 2 * n, add, jnp.zeros((rows, 2 * wc), jnp.float32))
        parts.append(part.astype(up.dtype))
    up[...] = jnp.concatenate([p[:, :wc] for p in parts], axis=1)
    down[...] = jnp.concatenate([p[:, wc:] for p in parts], axis=1)
    halo = (has_next, has_prev, nxt, prv, up, down, back, ahead, hs, hr)
    halo_start(*halo)
    steps_b(1)
    steps_c(1)
    keep(1).wait()
    halo_wait(*halo)
    sent(0)
    sent(1)


def reduce_kernel(n, shift, norm, left, right, grad, whole0, whole1, out, both, edge, g0, g1, sa, ra,
                  rb, rc, rd, later, earlier, gs, as_, ar, bs, br, cs, cr, ds, dr, hs, hr):
    z, x, y, c = place()
    barrier = greet(n, z, x, y, c)
    has_next, has_prev, nxt, prv, near = line(n, shift, z, x, y, c)
    greet_line(barrier, has_next, has_prev, nxt, prv)
    rows, wc2 = edge.shape[1:]
    wc = wc2 // 2
    x1, y1 = flip(x, y, c, 1, 0)
    x2, y2 = flip(x, y, c, 0, 1)
    to_c, to_b, to_a = at(z, x1, y1, c), at(z, x2, y2, c), at(z, x, y, 1 - c)

    def zof(t):
        return (z + t + 1) % n

    def block(h, m, core):
        q = m // n
        fx, fy = flip(x, y, core, 1 - q % 2, 1 - q // 2)
        s, f = at(zof(m % n), fx, fy, core)
        if h == 0:
            return jnp.dot(left[s], right[f], preferred_element_type=jnp.float32)
        return jnp.dot(left[s, :, :rows], edge[f], preferred_element_type=jnp.float32)

    load0 = pltpu.make_async_copy(whole0, g0, gs.at[0])
    load1 = pltpu.make_async_copy(whole1, g1, gs.at[1])
    load0.start()
    load1.start()
    sa[0, 0] = block(0, 0, 1 - c).astype(sa.dtype)
    pl.semaphore_wait(barrier, 3 + n - 1 + near)
    halo = (has_next, has_prev, nxt, prv, grad, grad, earlier, later, hs, hr)

    def copy_a(h, m):
        return remote(sa.at[h, m], ra.at[h, m], as_.at[h, m], ar.at[h, m], to_a)

    def copy_b(h, m):
        return remote(ra.at[h, m], rb.at[h, m], bs.at[h, m], br.at[h, m], to_b)

    def copy_c(h, j):
        return remote(ra.at[h, 2 * n + j], rc.at[h, j], cs.at[h, j], cr.at[h, j], to_c)

    def copy_d(h, t):
        return remote(ra.at[h, 3 * n + t], rd.at[h, t], ds.at[h, t], dr.at[h, t],
                      at(zof(t), x, y, c))

    def sends(h, first):
        def f(m):
            sa[h, m] = block(h, m, 1 - c).astype(sa.dtype)
            copy_a(h, m).start()

        loop(first, 4 * n, f)

    def steps_b(h):
        def f(m):
            mine = block(h, m, c)
            copy_a(h, m).wait_recv()
            ra[h, m] = (ra[h, m].astype(jnp.float32) + mine).astype(ra.dtype)
            copy_b(h, m).start()

        loop(0, 2 * n, f)

    def three(h, m):
        mine = block(h, 2 * n + m, c)
        copy_a(h, 2 * n + m).wait_recv()
        copy_b(h, m).wait_recv()
        return ra[h, 2 * n + m].astype(jnp.float32) + mine + rb[h, m].astype(jnp.float32)

    def steps_c(h):
        def f(j):
            ra[h, 2 * n + j] = three(h, j).astype(ra.dtype)
            copy_c(h, j).start()

        loop(0, n, f)

    def steps_d(h):
        def f(t):
            part = three(h, n + t)
            copy_c(h, t).wait_recv()
            ra[h, 3 * n + t] = (part + rc[h, t].astype(jnp.float32)).astype(ra.dtype)
            copy_d(h, t).start()

        loop(0, n - 1, f)
        part = three(h, 2 * n - 1)
        copy_c(h, n - 1).wait_recv()
        out[h] = part + rc[h, n - 1].astype(jnp.float32)

    def steps_out(h):
        def f(t):
            copy_d(h, t).wait_recv()
            out[h] += rd[h, t].astype(jnp.float32)

        loop(0, n - 1, f)
        out[h] = out[h] * norm

    copy_a(0, 0).start()
    halo_start(*halo)
    sends(0, 1)
    steps_b(0)
    halo_wait(*halo)
    for f in range(4):
        cols = slice(f * wc, (f + 1) * wc)
        edge[f] = jnp.concatenate([later[:, cols], earlier[:, cols]], axis=1)
    sends(1, 0)
    steps_c(0)
    steps_b(1)
    steps_d(0)
    steps_c(1)
    steps_d(1)
    load0.wait()
    load1.wait()
    tile = 256
    against = (((1,), (1,)), ((), ()))

    def product(t):
        where = pl.ds(pl.multiple_of(t * tile, tile), tile)
        total = jnp.zeros((2 * rows, tile), jnp.float32)
        sides = jnp.zeros((rows, tile), jnp.float32)
        for f in range(4):
            total += lax.dot_general(right[f], g1[f, where, :], against,
                                     preferred_element_type=jnp.float32)
            sides += lax.dot_general(edge[f], g0[f, where, :], against,
                                     preferred_element_type=jnp.float32)
        both[:rows, where] = total[:rows] + sides
        both[rows:, where] = total[rows:]

    loop(0, both.shape[1] // tile, product)
    steps_out(0)
    steps_out(1)
    for h in range(2):
        loop(0, 4 * n, lambda m: copy_a(h, m).wait_send())
        loop(0, 2 * n, lambda m: copy_b(h, m).wait_send())
        loop(0, n, lambda m: copy_c(h, m).wait_send())
        loop(0, n - 1, lambda m: copy_d(h, m).wait_send())


def body(inputs, cotangent, dilated_kernel_weight, point_weight):
    seqs, bins, width = inputs.shape
    peers, cols = lax.axis_size("seq"), lax.axis_size("fsdp")
    n = peers // 2
    shift = 128 // bins
    rows = seqs * bins
    norm_factor = 1.0 / math.sqrt(rows * peers * cols)
    wr, _, wc = dilated_kernel_weight.shape
    span = cols * wc
    bf, f32 = jnp.bfloat16, jnp.float32
    pack0 = jnp.concatenate([dilated_kernel_weight[:, 0], dilated_kernel_weight[:, 2]], axis=1)
    pack1 = jnp.concatenate([dilated_kernel_weight[:, 1], point_weight], axis=1)
    x = inputs.astype(f32).reshape(rows, width)
    cot = cotangent.reshape(rows, width)
    scale = lax.rsqrt(jnp.mean(x * x, axis=-1, keepdims=True) + 1e-06)
    normed = x * scale
    acts = gelu_value(normed).astype(bf)
    split = acts.reshape(rows, peers, wr).transpose(1, 0, 2)
    sem = lambda *k: pltpu.SemaphoreType.DMA(k)
    anyspec = pl.BlockSpec(memory_space=pl.ANY)
    vspec = pl.BlockSpec(memory_space=pltpu.VMEM)
    half = jax.ShapeDtypeStruct((cols, peers, wr, 2 * wc), bf)
    halo = jax.ShapeDtypeStruct((rows, span), bf)
    full0, full1, back, ahead = pl.pallas_call(
        functools.partial(gather_kernel, n, shift),
        out_shape=(half, half, halo, halo),
        in_specs=[anyspec, anyspec, vspec],
        out_specs=[vspec, anyspec, vspec, vspec],
        scratch_shapes=[pltpu.VMEM((rows, span), bf), pltpu.VMEM((rows, span), bf),
                        sem(2), sem(2, n), sem(2, n), sem(2, n), sem(2, n), sem(2, 2 * n),
                        sem(2, 2 * n), sem(2, 4 * n), sem(2, 4 * n), sem(2), sem(2)],
        compiler_params=pltpu.CompilerParams(
            collective_id=0, has_side_effects=True, vmem_limit_bytes=40 * 1024 * 1024),
    )(pack0, pack1, split)
    full0 = full0.reshape(cols, width, 2 * wc)
    full1 = full1.reshape(cols, width, 2 * wc)
    stacked = jnp.concatenate([acts, cot], axis=0)
    prod = [jnp.dot(stacked, full1[f], preferred_element_type=f32) for f in range(cols)]
    hidden = (jnp.concatenate([p[:rows, :wc] for p in prod], axis=1)
              + back.astype(f32) + ahead.astype(f32))
    back_mid = jnp.concatenate([p[rows:, wc:] for p in prod], axis=1)
    mid = gelu_value(hidden).astype(bf)
    grad = (back_mid * gelu_slope(hidden)).astype(bf)
    none = jnp.zeros((rows, wc), bf)
    right = jnp.stack([
        jnp.concatenate([
            jnp.concatenate([grad[:, f * wc:(f + 1) * wc], none], axis=1),
            jnp.concatenate([none, mid[:, f * wc:(f + 1) * wc]], axis=1)], axis=0)
        for f in range(cols)])
    left = stacked.T.reshape(peers, wr, 2 * rows)
    slot = lambda k: pltpu.VMEM((2, k, wr, 2 * wc), bf)
    reduced, both = pl.pallas_call(
        functools.partial(reduce_kernel, n, shift, norm_factor),
        out_shape=(jax.ShapeDtypeStruct((2, wr, 2 * wc), f32),
                   jax.ShapeDtypeStruct((2 * rows, width), f32)),
        in_specs=[vspec, vspec, vspec, anyspec, anyspec],
        out_specs=[vspec, vspec],
        scratch_shapes=[pltpu.VMEM((cols, rows, 2 * wc), bf), pltpu.VMEM(full0.shape, bf),
                        pltpu.VMEM(full1.shape, bf), slot(4 * n), slot(4 * n), slot(2 * n), slot(n), slot(n - 1),
                        pltpu.VMEM((rows, span), bf), pltpu.VMEM((rows, span), bf),
                        sem(2), sem(2, 4 * n), sem(2, 4 * n), sem(2, 2 * n), sem(2, 2 * n), sem(2, n),
                        sem(2, n), sem(2, n - 1), sem(2, n - 1), sem(2), sem(2)],
        compiler_params=pltpu.CompilerParams(
            collective_id=1, has_side_effects=True, vmem_limit_bytes=52 * 1024 * 1024),
    )(left, right, grad, full0, full1)
    outputs = (x + both[rows:]).astype(bf).reshape(seqs, bins, width)
    grad_normed = both[:rows] * gelu_slope(normed)
    inner = jnp.mean(grad_normed * x, axis=-1, keepdims=True)
    grad_inputs = (
        cot.astype(f32) + scale * (grad_normed - x * scale * scale * inner)
    ).astype(bf).reshape(seqs, bins, width)
    grad_conv = jnp.stack([reduced[1, :, :wc], reduced[0, :, :wc], reduced[1, :, wc:]], axis=1)
    grad_point = reduced[0, :, wc:]
    return (outputs, grad_inputs, grad_conv, grad_point)


def solution(mesh):
    specs = (
        P(None, ("seq", "fsdp"), None),
        P(None, ("seq", "fsdp"), None),
        P("seq", None, "fsdp"),
        P("seq", "fsdp"),
    )
    return jax.shard_map(body, mesh=mesh, in_specs=specs, out_specs=specs, check_vma=False)
```
